256 devices in a mesh: space: 32 (over x, z), grp: 8 (over y, core).
Axes of the slice: x: 4, y: 4, z: 8, core: 2. Of those that a mesh axis runs over, the one named last changes fastest.
Arguments:
- trial: bfloat16 [32768, 512], P(('space', 'grp')), may hold values from -11 to 11, as said below
- support: int32 [256, 2], P(('space', 'grp')), may hold values 0 or 1
- density: bfloat16 [32768, 1024], P(('space', 'grp')), may hold values from -0.25 to 0.25
- density_pattern: int32 [256, 8], P(('space', 'grp')), may hold values 0 or 1
- margin: bfloat16 [32768, 3072], P(('space', 'grp')), may hold values from -1 to 1, as said below
- margin_pattern: int32 [256, 24], P(('space', 'grp')), may hold values from 0 to 1, as said below
- pair_pattern: int32 [32, 3, 2, 2], P('space'), may hold values from 0 to 1, as said below
Outputs:
- orthonormal: float32 [32768, 1536], P(('space', 'grp'))
The draws below stay inside these ranges and needn't reach their ends.
Inputs may be any that keep to these rules, and one draw needn't show every extreme that they name: trial is a float array; its rows of later domains tend to be larger. margin, read with margin_pattern, is a symmetric matrix over all 32768 orbitals with unit diagonal. `margin_pattern`: symmetric between atom blocks over all domains; every atom block is paired with itself. `pair_pattern`: symmetric between trial blocks over all domains; every trial block is paired with itself.
All inputs are finite; a program needn't handle non-finite values. No bound on the sum of `support` or of `density_pattern` on one device may be relied on, other than what follows from the above.
Results may differ from the reference program's by a relative error of at most 0.004.
Values may be sent and summed in bfloat16 or wider, within the bound.
No kernel may reach another device: no remote copies, remote signals or barrier semaphores. Data moves between devices by JAX's collectives and lax.ppermute only.
A program may use at most 64 MiB of HBM per device.

```python
import math
import jax
import jax.numpy as jnp
from jax import lax

ATOM_ORBS = 128
TRIAL_WIDTH = 256
TRIALS = 2
DOM_ATOMS = 8
DOM_ROWS = 1024
DOMAINS = 32
ALL_ATOMS = 256
ORBITALS = 32768
TRIAL_COLS = 512


def draw_trial(key, part):
    base = jnp.clip(jax.random.normal(key, (ORBITALS, TRIAL_COLS), jnp.float32), -6.0, 6.0)
    domain = (jnp.arange(ORBITALS) // DOM_ROWS).astype(jnp.float32)
    ramp = 1.0 + 0.8 * domain / max(DOMAINS - 1, 1)
    return (base * ramp[:, None]).astype(jnp.bfloat16)


def draw_margin(key, part):
    key_inner, key_cross = jax.random.split(key)
    shape = (DOMAINS, DOM_ROWS, DOM_ROWS)
    inner = jnp.clip(jax.random.normal(key_inner, shape, jnp.float32), -6.0, 6.0)
    cross = jnp.clip(jax.random.normal(key_cross, shape, jnp.float32), -6.0, 6.0)
    spread = 0.35 / math.sqrt(1.5 * DOM_ROWS)
    identity = jnp.eye(DOM_ROWS, dtype=jnp.float32)[None]
    inner = (inner + jnp.swapaxes(inner, 1, 2)) * (spread / math.sqrt(2.0))
    inner = inner * (1.0 - identity) + identity
    cross = cross * (4.0 * spread)
    before = jnp.swapaxes(jnp.roll(cross, 1, axis=0), 1, 2)
    whole = jnp.concatenate([before, inner, cross], axis=2)
    return whole.reshape(ORBITALS, 3 * DOM_ROWS).astype(jnp.bfloat16)


def draw_margin_pattern(key, part):
    key_inner, key_cross = jax.random.split(key)
    inner = jax.random.randint(key_inner, (DOMAINS, DOM_ATOMS, DOM_ATOMS), 0, 2, dtype=jnp.int32)
    inner = jnp.maximum(inner, jnp.swapaxes(inner, 1, 2))
    inner = jnp.maximum(inner, jnp.eye(DOM_ATOMS, dtype=jnp.int32)[None])
    cross = jax.random.randint(key_cross, (DOMAINS, DOM_ATOMS, DOM_ATOMS), 0, 2, dtype=jnp.int32)
    before = jnp.swapaxes(jnp.roll(cross, 1, axis=0), 1, 2)
    whole = jnp.concatenate([before, inner, cross], axis=2)
    return whole.reshape(ALL_ATOMS, 3 * DOM_ATOMS).astype(jnp.int32)


def draw_pair_pattern(key, part):
    key_inner, key_cross = jax.random.split(key)
    inner = jax.random.randint(key_inner, (DOMAINS, TRIALS, TRIALS), 0, 2, dtype=jnp.int32)
    inner = jnp.maximum(inner, jnp.swapaxes(inner, 1, 2))
    inner = jnp.maximum(inner, jnp.eye(TRIALS, dtype=jnp.int32)[None])
    cross = jax.random.randint(key_cross, (DOMAINS, TRIALS, TRIALS), 0, 2, dtype=jnp.int32)
    before = jnp.swapaxes(jnp.roll(cross, 1, axis=0), 1, 2)
    return jnp.stack([before, inner, cross], axis=1).astype(jnp.int32)


def touch_ends(drawn, own_key, low, top_value):
    longest = drawn.shape.index(max(drawn.shape))
    spots = []
    for shift in (0, 1):
        where = [jax.random.randint(jax.random.fold_in(own_key, axis), (), 0, length) for axis, length in enumerate(drawn.shape)]
        where[longest] = (where[longest] + shift) % drawn.shape[longest]
        spots.append(tuple(where))
    return drawn.at[spots[0]].set(low).at[spots[1]].set(top_value)


def block_levels(stream_key, dims, cuts, least, top_value):
    def one(position, shards_of):
        draws = jax.random.uniform(jax.random.fold_in(jax.random.fold_in(stream_key, 6), position), (shards_of,), jnp.float32, least / len(cuts), top_value / len(cuts))
        return jnp.repeat(jnp.exp(draws), dims[position] // shards_of).reshape((-1,) + (1,) * (len(dims) - position - 1))

    gain = one(*cuts[0])
    for cut in cuts[1:]:
        gain = gain * one(*cut)
    return gain


def centred(rng, extent, width, reach, shards=(), held_as=jnp.bfloat16):
    drawn = width * jax.random.normal(rng, extent, jnp.float32)
    if shards:
        drawn = drawn * block_levels(rng, extent, shards, -0.22, 0.18)
    return jnp.clip(drawn, -reach, reach).astype(held_as)


def setup_inputs(seed: int = 0) -> dict:
    keys = jax.random.split(jax.random.key(seed), 8)
    trial = draw_trial(jax.random.fold_in(keys[7], 71), 0)
    support = touch_ends((jax.random.randint(keys[1], (ALL_ATOMS, TRIALS), 0, 3) < 2).astype(jnp.int32), jax.random.fold_in(keys[1], 1), 0, 1)
    density = centred(keys[2], (ORBITALS, DOM_ROWS), (DOM_ROWS // 2) ** -0.5, 0.25, ((0, 256),))
    density_pattern = touch_ends((jax.random.randint(keys[3], (ALL_ATOMS, DOM_ATOMS), 0, 2) < 1).astype(jnp.int32), jax.random.fold_in(keys[3], 1), 0, 1)
    margin = draw_margin(jax.random.fold_in(keys[7], 71), 0)
    margin_pattern = draw_margin_pattern(jax.random.fold_in(keys[7], 71), 0)
    pair_pattern = draw_pair_pattern(jax.random.fold_in(keys[7], 71), 0)
    return dict(trial=trial, support=support, density=density, density_pattern=density_pattern, margin=margin, margin_pattern=margin_pattern, pair_pattern=pair_pattern)


def matmul_high(left_side, right_side):
    return jnp.einsum('sik,skj->sij', left_side, right_side, precision=lax.Precision.HIGHEST)


def band_product(left_side, right_side):
    before = jnp.roll(right_side, 1, axis=0)
    after = jnp.roll(right_side, -1, axis=0)
    lower = matmul_high(left_side[:, 0], before[:, 1]) + matmul_high(left_side[:, 1], right_side[:, 0])
    center = matmul_high(left_side[:, 0], before[:, 2]) + matmul_high(left_side[:, 1], right_side[:, 1]) + matmul_high(left_side[:, 2], after[:, 0])
    upper = matmul_high(left_side[:, 1], right_side[:, 2]) + matmul_high(left_side[:, 2], after[:, 1])
    return jnp.stack([lower, center, upper], axis=1)


def reference(trial, support, density, density_pattern, margin, margin_pattern, pair_pattern):
    support_mask = support.astype(jnp.bfloat16).reshape(ALL_ATOMS, 1, TRIALS, 1)
    trial_eff = (trial.reshape(ALL_ATOMS, ATOM_ORBS, TRIALS, TRIAL_WIDTH) * support_mask).reshape(DOMAINS, DOM_ROWS, TRIAL_COLS)
    density_mask = density_pattern.astype(jnp.bfloat16).reshape(ALL_ATOMS, 1, DOM_ATOMS, 1)
    density_eff = (density.reshape(ALL_ATOMS, ATOM_ORBS, DOM_ATOMS, ATOM_ORBS) * density_mask).reshape(DOMAINS, DOM_ROWS, DOM_ROWS)

    def project(operands):
        return jnp.dot(operands[0], operands[1], preferred_element_type=jnp.float32).astype(jnp.bfloat16)

    projected = lax.map(project, (density_eff, trial_eff))
    nearby = jnp.stack([jnp.roll(projected, 1, axis=0), projected, jnp.roll(projected, -1, axis=0)], axis=1)

    def margin_rows(arrays):
        values, pattern, near_psi, own_psi = arrays
        masked = values.reshape(DOM_ATOMS, ATOM_ORBS, 3, DOM_ATOMS, ATOM_ORBS) * pattern.astype(jnp.bfloat16).reshape(DOM_ATOMS, 1, 3, DOM_ATOMS, 1)
        masked = masked.reshape(DOM_ROWS, 3, DOM_ROWS)
        applied = jnp.einsum('rjc,jct->jrt', masked.astype(jnp.float32), near_psi.astype(jnp.float32)).astype(jnp.bfloat16)
        return jnp.einsum('rt,jru->jtu', own_psi.astype(jnp.float32), applied.astype(jnp.float32))

    blocks = lax.map(margin_rows, (margin.reshape(DOMAINS, DOM_ROWS, 3 * DOM_ROWS), margin_pattern.reshape(DOMAINS, DOM_ATOMS, 3 * DOM_ATOMS), nearby, projected))
    pair_mask = jnp.broadcast_to(pair_pattern.astype(jnp.float32).reshape(DOMAINS, 3, TRIALS, 1, TRIALS, 1), (DOMAINS, 3, TRIALS, TRIAL_WIDTH, TRIALS, TRIAL_WIDTH)).reshape(DOMAINS, 3, TRIAL_COLS, TRIAL_COLS)
    blocks = blocks * pair_mask
    peak = jnp.max(jnp.diagonal(blocks[:, 1], axis1=1, axis2=2))
    scaled = blocks / peak
    identity = jnp.eye(TRIAL_COLS, dtype=jnp.float32)
    nothing = jnp.zeros_like(identity)
    identity_band = jnp.stack([nothing, identity, nothing])[None]
    z_one = pair_mask * (1.5 * identity_band - 0.5 * scaled)
    square = pair_mask * band_product(z_one, z_one)
    weighed = pair_mask * band_product(scaled, square)
    z_two = pair_mask * (1.5 * z_one - 0.5 * band_product(z_one, weighed))
    result = jnp.einsum('srt,sjtu->srju', projected.astype(jnp.float32), z_two, precision=lax.Precision.HIGHEST)
    return result.reshape(ORBITALS, 3 * TRIAL_COLS)
```

```python
import jax
import jax.numpy as jnp
from jax import lax
from jax.experimental import pallas as pl
from jax.experimental.pallas import tpu as pltpu
from jax.sharding import PartitionSpec as P

BF = jnp.bfloat16
F32 = jnp.float32
ATOM = 128
WIDTH = 256
COLS = 512
ROWS = 1024
CHIP_ROWS = 256
LEVELS = 4
HIGH = 48 * 1024 * 1024


def here():
    grp = lax.axis_index("grp")
    return grp // 2, lax.rem(grp, 2)


def dot(left, right):
    return jnp.dot(left, right, preferred_element_type=F32)


def keep_if(flag, block):
    return jnp.where(flag != 0, block, jnp.zeros_like(block))


def smem():
    return pl.BlockSpec(memory_space=pltpu.SMEM)


def vmem():
    return pl.BlockSpec(memory_space=pltpu.VMEM)


def call(body, outs, ins, specs, scratch=(), flops=0):
    size = sum(x.size * x.dtype.itemsize for x in ins) + sum(
        o.size * o.dtype.itemsize for o in outs
    )
    return pl.pallas_call(
        body,
        out_shape=outs,
        in_specs=specs,
        out_specs=[vmem() for _ in outs],
        scratch_shapes=list(scratch),
        compiler_params=pltpu.CompilerParams(vmem_limit_bytes=HIGH),
        cost_estimate=pl.CostEstimate(flops=flops, bytes_accessed=size, transcendentals=0),
    )(*ins)


def shape(rows, cols, dtype=BF):
    return jax.ShapeDtypeStruct((rows, cols), dtype)


def shift(array, axis, by):
    n = lax.axis_size(axis)
    return lax.ppermute(array, axis, [(i, (i + by) % n) for i in range(n)])


def swap_core(array):
    n = lax.axis_size("grp")
    return lax.ppermute(array, "grp", [(i, i ^ 1) for i in range(n)])


def along_y(array):
    return [shift(array, "grp", -2), shift(array, "grp", 4), shift(array, "grp", 2)]


def mask_trial(support, trial, out):
    for t in range(2):
        cols = slice(t * WIDTH, (t + 1) * WIDTH)
        out[:, cols] = keep_if(support[0, t], trial[:, cols])


def mask_rows(dens_pat, marg_pat, dens, marg, dens_own, dens_pair, marg_out):
    y, core = here()
    for k in range(LEVELS):
        for side, target in ((core, dens_own), (1 - core, dens_pair)):
            block = lax.rem(y + k, LEVELS) * 2 + side
            start = pl.multiple_of(block * ATOM, ATOM)
            target[:, k * ATOM : (k + 1) * ATOM] = keep_if(
                dens_pat[0, block], dens[:, pl.ds(start, ATOM)]
            )
    for b in range(16):
        cols = slice(b * ATOM, (b + 1) * ATOM)
        marg_out[:, cols] = keep_if(marg_pat[0, b], marg[:, cols])


def project(dens_own, dens_pair, t0, t1, t2, t3, kept, sent):
    y, core = here()
    stacked = jnp.concatenate([t0[...], t1[...], t2[...], t3[...]], axis=0)
    for dens, rows in ((dens_own, core), (dens_pair, 1 - core)):
        part = dot(dens[...], stacked)
        low, high = part[:, :WIDTH], part[:, WIDTH:]
        at = pl.ds(pl.multiple_of(rows * ATOM, ATOM), ATOM)
        kept[at, :] = jnp.where(core == 0, low, high)
        sent[at, :] = jnp.where(core == 0, high, low)


def gram(
    pair, p0, p1, p2, p3, q0, q1, q2, q3, other, m_own, m_pair,
    kept, s1, s2, s3, rows_out, own, near, left, marg,
):
    y, core = here()
    for k, (p, q) in enumerate(((p0, q0), (p1, q1), (p2, q2), (p3, q3))):
        at = pl.ds(pl.multiple_of(lax.rem(y + k, LEVELS) * CHIP_ROWS, CHIP_ROWS), CHIP_ROWS)
        own[at, :] = p[...]
        near[at, :] = q[...]
    left[:, pl.ds(pl.multiple_of(core * WIDTH, WIDTH), WIDTH)] = p0[...]
    left[:, pl.ds(pl.multiple_of((1 - core) * WIDTH, WIDTH), WIDTH)] = other[...]
    marg[pl.ds(pl.multiple_of(core * ATOM, ATOM), ATOM), :] = m_own[...]
    marg[pl.ds(pl.multiple_of((1 - core) * ATOM, ATOM), ATOM), :] = m_pair[...]
    rows_out[...] = left[pl.ds(pl.multiple_of(core * ATOM, ATOM), ATOM), :]
    applied_own = dot(marg[:, ROWS:], own[...]).astype(BF)
    applied_near = dot(marg[:, :ROWS], near[...]).astype(BF)
    diag = jnp.sum(p0[...].astype(F32) * applied_own.astype(F32), axis=0, keepdims=True)
    high = diag.astype(BF).astype(F32)
    row = lax.broadcasted_iota(jnp.int32, (16, WIDTH), 0)
    tail = jnp.where(row == 0, high, jnp.where(row == 1, diag - high, 0.0))
    for k, out in enumerate((kept, s1, s2, s3)):
        chunk = lax.rem(y + k, LEVELS)
        lanes = pl.ds(pl.multiple_of(chunk * ATOM, ATOM), ATOM)
        rows = left[:, lanes].T
        own_flag = pair[0, 1, chunk // 2, core]
        near_flag = pair[0, 0, chunk // 2, core]
        out[:ATOM, :] = keep_if(own_flag, dot(rows, applied_own)).astype(out.dtype)
        out[ATOM : 2 * ATOM, :] = keep_if(near_flag, dot(rows, applied_near)).astype(out.dtype)
        out[2 * ATOM :, :] = tail.astype(out.dtype)


def add_parts(kept, s1, s2, s3, shard, own_out, peak):
    total = kept[...]
    for s in (s1, s2, s3):
        total = total + s[...].astype(F32)
    shard[...] = total[: 2 * ATOM].astype(BF)
    own_out[...] = total[:ATOM].astype(BF)
    diag = jnp.sum(total[2 * ATOM :], axis=0, keepdims=True)
    peak[...] = jnp.full((8, 128), jnp.max(diag), F32)


def purify(
    pair, peak, own_mine, own_pair, near_mine, near_pair, row_before, row_here, row_after,
    to_before, here_out, to_after, band, power, total,
):
    y, core = here()
    level = jnp.max(peak[...])
    ones = jnp.full((8, 128), level, F32)
    scale = jnp.max(jnp.exp2(-jnp.floor(jnp.log2(jnp.abs(ones)))))
    inverse = jnp.max(1.0 / (ones * scale))

    def place(row, col, block, side, k):
        chunk = lax.rem(y + k, LEVELS)
        at = pl.ds(pl.multiple_of(row * COLS + chunk * ATOM, ATOM), ATOM)
        lanes = pl.ds(pl.multiple_of(col * COLS + side * WIDTH, WIDTH), WIDTH)
        band[at, lanes] = (block.astype(F32) * scale).astype(BF)

    for own, near, side in ((own_mine, near_mine, core), (own_pair, near_pair, 1 - core)):
        for k in range(LEVELS):
            base = k * 2 * ATOM
            place(1, 1, own[base : base + ATOM, :], side, k)
            place(1, 0, own[base + ATOM : base + 2 * ATOM, :], side, k)
            base = k * 3 * ATOM
            place(0, 0, near[base : base + ATOM, :], side, k)
            place(2, 2, near[base + ATOM : base + 2 * ATOM, :], side, k)
            place(2, 1, near[base + 2 * ATOM : base + 3 * ATOM, :], side, k)
    band[:COLS, COLS : 2 * COLS] = band[COLS : 2 * COLS, :COLS].T
    band[COLS : 2 * COLS, 2 * COLS :] = band[2 * COLS :, COLS : 2 * COLS].T

    row = lax.broadcasted_iota(jnp.int32, (ATOM, ATOM), 0)
    col = lax.broadcasted_iota(jnp.int32, (ATOM, ATOM), 1)
    on_diag = row == col
    gathered = jnp.zeros((ATOM, ATOM), F32)
    for b in range(LEVELS):
        at = slice(COLS + b * ATOM, COLS + (b + 1) * ATOM)
        gathered = gathered + jnp.where(on_diag, band[at, at].astype(F32), 0.0)
    mean = jnp.full((16, 128), jnp.sum(gathered) * (1.0 / COLS), F32)
    centre = jnp.max(mean.astype(BF).astype(F32))
    for b in range(3 * LEVELS):
        at = slice(b * ATOM, (b + 1) * ATOM)
        block = band[at, at].astype(F32)
        band[at, at] = jnp.where(on_diag, block - centre, block).astype(BF)

    c = inverse
    x = centre * c
    g0 = 2.25 + x * (-2.4375 + x * (1.6875 + x * (-0.5625 + x * 0.0625)))
    g1 = (-2.4375 + x * (3.375 + x * (-1.6875 + x * 0.25))) * c
    g2 = (1.6875 + x * (-1.6875 + x * 0.375)) * c * c
    g3 = (-0.5625 + x * 0.25) * c * c * c
    g4 = 0.0625 * c * c * c * c

    power[0] = band[:, COLS : 2 * COLS]
    total[...] = g1 * power[0].astype(F32)

    def step(n, carry):
        gain = jnp.where(n == 0, g2, jnp.where(n == 1, g3, g4))
        source = lax.rem(n, 2)
        for r in range(3):
            first, last = max(r - 1, 0) * COLS, min(r + 2, 3) * COLS
            product = dot(band[r * COLS : (r + 1) * COLS, first:last], power[source, first:last, :])
            for t in range(2):
                for u in range(2):
                    flag = pair[0, 1, t, u] if r == 1 else pair[0, r, u, t]
                    part = keep_if(
                        flag,
                        product[t * WIDTH : (t + 1) * WIDTH, u * WIDTH : (u + 1) * WIDTH],
                    )
                    at = slice(r * COLS + t * WIDTH, r * COLS + (t + 1) * WIDTH)
                    lanes = slice(u * WIDTH, (u + 1) * WIDTH)
                    power[1 - source, at, lanes] = part.astype(BF)
                    total[at, lanes] += gain * part
        return carry

    lax.fori_loop(0, 3, step, 0)
    to_before[...] = dot(row_before[...], total[:COLS].astype(BF)).astype(BF)
    here_out[...] = g0 * row_here[...].astype(F32) + dot(
        row_here[...], total[COLS : 2 * COLS].astype(BF)
    )
    to_after[...] = dot(row_after[...], total[2 * COLS :].astype(BF)).astype(BF)


def assemble(before, own, after, out):
    out[:, :COLS] = before[...].astype(F32)
    out[:, COLS : 2 * COLS] = own[...]
    out[:, 2 * COLS :] = after[...].astype(F32)


def per_device(trial, support, density, density_pattern, margin, margin_pattern, pair_pattern):
    (slab,) = call(mask_trial, [shape(ATOM, COLS)], [support, trial], [smem(), vmem()])
    slabs = along_y(slab)
    dens_own, dens_pair, marg = pl.pallas_call(
        mask_rows,
        out_shape=[shape(ATOM, COLS), shape(ATOM, COLS), shape(ATOM, 2 * ROWS)],
        grid=(1,),
        in_specs=[
            smem(),
            smem(),
            pl.BlockSpec((ATOM, ROWS), lambda i: (0, 0)),
            pl.BlockSpec((ATOM, 2 * ROWS), lambda i: (0, 0)),
        ],
        out_specs=[
            pl.BlockSpec((ATOM, COLS), lambda i: (0, 0)),
            pl.BlockSpec((ATOM, COLS), lambda i: (0, 0)),
            pl.BlockSpec((ATOM, 2 * ROWS), lambda i: (0, 0)),
        ],
        compiler_params=pltpu.CompilerParams(vmem_limit_bytes=HIGH),
        cost_estimate=pl.CostEstimate(flops=0, bytes_accessed=2 * 2**20, transcendentals=0),
    )(density_pattern, margin_pattern, density, margin)
    dens_got = swap_core(dens_pair)
    marg_got = swap_core(marg)
    kept, sent = call(
        project,
        [shape(CHIP_ROWS, WIDTH, F32), shape(CHIP_ROWS, WIDTH, F32)],
        [dens_own, dens_got, slab, *slabs],
        [vmem()] * 6,
        flops=2 * 256 * 512 * 512,
    )
    projected = (kept + swap_core(sent)).astype(BF)
    near = shift(projected, "space", 1)
    own_pieces = along_y(projected)
    other = swap_core(projected)
    near_pieces = along_y(near)
    tail = 2 * ATOM + 16
    kept, s1, s2, s3, rows_here = call(
        gram,
        [shape(tail, WIDTH, F32)] + [shape(tail, WIDTH)] * 3 + [shape(ATOM, COLS)],
        [pair_pattern, projected, *own_pieces, near, *near_pieces, other, marg, marg_got],
        [smem()] + [vmem()] * 11,
        scratch=[
            pltpu.VMEM((ROWS, WIDTH), BF),
            pltpu.VMEM((ROWS, WIDTH), BF),
            pltpu.VMEM((CHIP_ROWS, COLS), BF),
            pltpu.VMEM((CHIP_ROWS, 2 * ROWS), BF),
        ],
        flops=2 * 256 * 256 * (2048 + 1024),
    )
    got = [shift(s1, "grp", 2), shift(s2, "grp", 4), shift(s3, "grp", -2)]
    shard, own_shard, peak = call(
        add_parts,
        [shape(2 * ATOM, WIDTH), shape(ATOM, WIDTH), shape(8, 128, F32)],
        [kept, *got],
        [vmem()] * 4,
    )
    below = shift(own_shard, "space", 1)
    above = shift(shard, "space", -1)
    own_band = jnp.concatenate([shard, *along_y(shard)], axis=0)
    own_band_pair = swap_core(own_band)
    near_shard = jnp.concatenate([below, above], axis=0)
    near_band = jnp.concatenate([near_shard, *along_y(near_shard)], axis=0)
    near_band_pair = swap_core(near_band)
    peak = jnp.maximum(peak, swap_core(peak))
    for by in (1, 3, 9):
        peak = jnp.maximum(
            peak, jnp.maximum(shift(peak, "space", by), shift(peak, "space", -by))
        )
    peak = jnp.maximum(peak, shift(peak, "space", 5))
    rows_before = shift(rows_here, "space", 1)
    rows_after = shift(rows_here, "space", -1)
    to_before, result, to_after = call(
        purify,
        [shape(ATOM, COLS), shape(ATOM, COLS, F32), shape(ATOM, COLS)],
        [
            pair_pattern, peak, own_band, own_band_pair, near_band, near_band_pair,
            rows_before, rows_here, rows_after,
        ],
        [smem()] + [vmem()] * 8,
        scratch=[
            pltpu.VMEM((3 * COLS, 3 * COLS), BF),
            pltpu.VMEM((2, 3 * COLS, COLS), BF),
            pltpu.VMEM((3 * COLS, COLS), F32),
        ],
        flops=2 * 21 * 512**3,
    )
    before = shift(to_after, "space", 1)
    after = shift(to_before, "space", -1)
    (out,) = call(
        assemble, [shape(ATOM, 3 * COLS, F32)], [before, result, after], [vmem()] * 3
    )
    return out


def solution(mesh):
    placed = (
        P(("space", "grp"), None),
        P(("space", "grp"), None),
        P(("space", "grp"), None),
        P(("space", "grp"), None),
        P(("space", "grp"), None),
        P(("space", "grp"), None),
        P("space", None, None, None),
    )
    return jax.shard_map(
        per_device, mesh=mesh, in_specs=placed, out_specs=P(("space", "grp"), None), check_vma=False
    )
```
